32 devices in a mesh: blk: 8 (over y, x, core), space: 4 (over z).
Axes of the slice: x: 2, y: 2, z: 4, core: 2. Of those that a mesh axis runs over, the one named last changes fastest.
Arguments:
- input_field: bfloat16 [128, 96, 96, 192], P('blk', 'space'), may hold values from -6 to 6
- cotangent: bfloat16 [128, 96, 96, 192], P('blk', 'space'), may hold values from -0.59765625 to 0.59765625
- weights: bfloat16 [16, 32, 8, 2, 128, 128], P('space', 'blk'), may hold values from -0.375 to 0.375
Outputs:
- spectral_out: bfloat16 [128, 96, 96, 192], P('blk', 'space')
- field_grad: bfloat16 [128, 96, 96, 192], P('blk', 'space')
- weight_grad: float32 [16, 32, 8, 2, 128, 128], P('space', 'blk')
The draws below stay inside these ranges and needn't reach their ends.
All inputs are finite; a program needn't handle non-finite values.
Results may differ from the reference program's by a relative error of at most 0.015.
Values may be sent and summed in bfloat16 or wider, within the bound.
A program may use at most 192 MiB of HBM per device.

```python
import math
import jax
import jax.numpy as jnp
from jax import lax

C = 128
NX = 96
NY = 192
NZ = 96
MX = 16
MY = 32
MZ = 8


def block_scale(own_key, dims, pieces, smallest, high):
    factor_of = 1.0
    for dim, blocks in pieces:
        draws = jax.random.uniform(jax.random.fold_in(jax.random.fold_in(own_key, 6), dim), (blocks,), jnp.float32, smallest / len(pieces), high / len(pieces))
        factor_of = factor_of * jnp.repeat(jnp.exp(draws), dims[dim] // blocks).reshape((-1,) + (1,) * (len(dims) - 1 - dim))
    return factor_of


def scatter_about(own_key, extent, spread, most, pieces=(), held_as=jnp.bfloat16):
    result = spread * jax.random.normal(own_key, extent, jnp.float32)
    if pieces:
        result = result * block_scale(own_key, extent, pieces, -0.22, 0.18)
    return jnp.clip(result, -most, most).astype(held_as)


def setup_inputs(seed: int = 0) -> dict:
    keys = jax.random.split(jax.random.key(seed), 4)
    return {
        "input_field": scatter_about(keys[0], (C, NZ, NX, NY), 1.0, 6.0, ((0, 8), (1, 4))),
        "cotangent": scatter_about(keys[1], (C, NZ, NX, NY), 0.1, 0.59765625, ((0, 8), (1, 4))),
        "weights": scatter_about(keys[2], (MX, MY, MZ, 2, C, C), (2 * C) ** -0.5, 0.375, ((0, 4), (1, 8))),
    }


def centered_freqs(total_count):
    indices = jnp.arange(total_count, dtype=jnp.int32)
    return jnp.where(indices < total_count // 2, indices, indices - total_count)

def phase_pair(frequencies, positions, length):
    product = frequencies[:, None] * positions[None, :] % length
    angles = product.astype(jnp.float32) * (2.0 * math.pi / length)
    return (jnp.cos(angles), jnp.sin(angles))

def x_analysis_table():
    cosines, sine_values = phase_pair(centered_freqs(MX), jnp.arange(NX, dtype=jnp.int32), NX)
    return jnp.stack([cosines.T, -sine_values.T], 1).astype(jnp.bfloat16)

def y_analysis_table():
    cosines, sine_values = phase_pair(centered_freqs(MY), jnp.arange(NY, dtype=jnp.int32), NY)
    real_rows = jnp.stack([cosines.T, -sine_values.T], 1)
    imag_rows = jnp.stack([sine_values.T, cosines.T], 1)
    return jnp.stack([real_rows, imag_rows], 0).astype(jnp.bfloat16)

def z_analysis_table(positions):
    cosines, sine_values = phase_pair(jnp.arange(MZ, dtype=jnp.int32), positions, NZ)
    real_rows = jnp.stack([cosines.T, -sine_values.T], 1)
    imag_rows = jnp.stack([sine_values.T, cosines.T], 1)
    return jnp.stack([real_rows, imag_rows], 0).astype(jnp.bfloat16)

def mode_weights():
    return jnp.where(jnp.arange(MZ) == 0, 1.0, 2.0).astype(jnp.float32)

def z_synthesis_table(positions, amplitude):
    cosines, sine_values = phase_pair(jnp.arange(MZ, dtype=jnp.int32), positions, NZ)
    cosines = cosines * amplitude[:, None]
    sine_values = sine_values * amplitude[:, None]
    real_rows = jnp.stack([cosines, sine_values], -1)
    imag_rows = jnp.stack([-sine_values, cosines], -1)
    return jnp.stack([real_rows, imag_rows], 1).astype(jnp.bfloat16)

def y_synthesis_table():
    cosines, sine_values = phase_pair(centered_freqs(MY), jnp.arange(NY, dtype=jnp.int32), NY)
    real_rows = jnp.stack([cosines, sine_values], 1)
    imag_rows = jnp.stack([-sine_values, cosines], 1)
    return jnp.stack([real_rows, imag_rows], 0).astype(jnp.bfloat16)

def x_synthesis_table():
    cosines, sine_values = phase_pair(centered_freqs(MX), jnp.arange(NX, dtype=jnp.int32), NX)
    return jnp.stack([cosines, -sine_values], 0).astype(jnp.bfloat16)

def contract(pattern, first_operand, second_operand):
    return jnp.einsum(pattern, first_operand.astype(jnp.float32), second_operand.astype(jnp.float32), precision=lax.Precision.HIGHEST)

def analyse(values, x_table, y_table):

    def one_group(channel_block):
        xsum = contract('czxy,xrp->czrpy', channel_block, x_table).astype(jnp.bfloat16)
        return contract('czrpy,ryoq->czopq', xsum, y_table).astype(jnp.bfloat16)
    groups = values.reshape(C // 8, 8, NZ, NX, NY)
    return lax.map(one_group, groups).reshape(C, NZ, 2, MX, MY)

def synthesize(zback, y_table, x_table):

    def one_group(channel_block):
        yback = contract('czipq,iqoy->czopy', channel_block, y_table).astype(jnp.bfloat16)
        return contract('czipy,ipx->czxy', yback, x_table).astype(jnp.bfloat16)
    groups = zback.reshape(C // 8, 8, NZ, 2, MX, MY)
    return lax.map(one_group, groups).reshape(C, NZ, NX, NY)

def reference(input_field, cotangent, weights):
    forward_scale = 1.0 / math.sqrt(NX * NY * NZ)
    synth_scale = 1.0 / math.sqrt(MX * MY * MZ)
    amplitude = mode_weights()
    x_table = x_analysis_table()
    y_table = y_analysis_table()
    plane_f = analyse(input_field, x_table, y_table)
    plane_g = analyse(cotangent, x_table, y_table)
    z_positions = jnp.arange(NZ, dtype=jnp.int32)
    z_table = z_analysis_table(z_positions)
    zsum_f = contract('czipq,izok->ckopq', plane_f, z_table)
    zsum_g = contract('czipq,izok->ckopq', plane_g, z_table)
    spec_f = (zsum_f * forward_scale).astype(jnp.bfloat16)
    spec_g = (zsum_g * (amplitude * synth_scale)[None, :, None, None, None]).astype(jnp.bfloat16)
    w_real = weights[:, :, :, 0]
    w_imag = weights[:, :, :, 1]
    f_real = spec_f[:, :, 0]
    f_imag = spec_f[:, :, 1]
    g_real = spec_g[:, :, 0]
    g_imag = spec_g[:, :, 1]
    mixed_real = contract('abkoc,ckab->okab', w_real, f_real) - contract('abkoc,ckab->okab', w_imag, f_imag)
    mixed_imag = contract('abkoc,ckab->okab', w_real, f_imag) + contract('abkoc,ckab->okab', w_imag, f_real)
    mixed = jnp.stack([mixed_real, mixed_imag], 2).astype(jnp.bfloat16)
    grad_real = contract('abkoc,okab->ckab', w_real, g_real) + contract('abkoc,okab->ckab', w_imag, g_imag)
    grad_imag = contract('abkoc,okab->ckab', w_real, g_imag) - contract('abkoc,okab->ckab', w_imag, g_real)
    grad_spec = jnp.stack([grad_real, grad_imag], 2).astype(jnp.bfloat16)
    wgrad_real = contract('okab,ckab->abkoc', g_real, f_real) + contract('okab,ckab->abkoc', g_imag, f_imag)
    wgrad_imag = contract('okab,ckab->abkoc', g_imag, f_real) - contract('okab,ckab->abkoc', g_real, f_imag)
    weight_grad = jnp.stack([wgrad_real, wgrad_imag], 3)
    unit_weights = jnp.ones((MZ,), jnp.float32)
    zback_y = (contract('ckipq,kizo->czopq', mixed, z_synthesis_table(z_positions, amplitude)) * synth_scale).astype(jnp.bfloat16)
    zback_u = (contract('ckipq,kizo->czopq', grad_spec, z_synthesis_table(z_positions, unit_weights)) * forward_scale).astype(jnp.bfloat16)
    y_back_table = y_synthesis_table()
    x_back_table = x_synthesis_table()
    spectral_out = synthesize(zback_y, y_back_table, x_back_table)
    field_grad = synthesize(zback_u, y_back_table, x_back_table)
    return (spectral_out, field_grad, weight_grad)
```

```python
import functools
import math

import jax
import jax.numpy as jnp
import numpy as np
from jax import lax
from jax.experimental import pallas as pl
from jax.experimental.pallas import tpu as pltpu
from jax.sharding import PartitionSpec as P

F32 = jnp.float32
BF16 = jnp.bfloat16


def centered_freqs(count):
    indices = np.arange(count, dtype=np.int64)
    return np.where(indices < count // 2, indices, indices - count)


def phase_pair(frequencies, positions, length):
    product = (frequencies[:, None] * positions[None, :]) % length
    angles = product.astype(np.float32) * np.float32(2.0 * math.pi / length)
    return np.cos(angles).astype(np.float32), np.sin(angles).astype(np.float32)


def rounded(table):
    return np.asarray(table, np.float32).astype(jnp.bfloat16)


def lane_slots(my):
    return max(1, 128 // my)


def lane_groups(my, local):
    return math.gcd(lane_slots(my), local)


def y_tables(ny, my, groups):
    cosines, sines = phase_pair(centered_freqs(my), np.arange(ny), ny)
    half = lane_slots(my) * my
    forward = np.zeros((groups, ny, 2 * half), np.float32)
    for i in range(groups):
        forward[i, :, i * my:(i + 1) * my] = cosines.T
        forward[i, :, half + i * my:half + (i + 1) * my] = -sines.T
    return rounded(forward), rounded(np.swapaxes(forward, 1, 2))


def x_tables(nx, mx):
    cosines, sines = phase_pair(centered_freqs(mx), np.arange(nx), nx)
    forward = np.concatenate([cosines, -sines], 0)
    backward = np.concatenate([cosines, sines], 0).T
    return rounded(forward), rounded(backward)


def z_tables(nz, mz, my, space_count, groups):
    cosines, sines = phase_pair(np.arange(mz), np.arange(nz), nz)
    local = nz // space_count
    per_group = local // groups
    amplitude = np.where(np.arange(mz) == 0, 1.0, 2.0).astype(np.float32)[:, None]

    def spread(weight):
        pair = np.stack([rounded(cosines * weight), rounded(sines * weight)], 1).astype(np.float32)
        pair = pair.reshape(mz, 2, space_count, groups, per_group)
        pair = pair.transpose(2, 4, 0, 1, 3)
        unused = (lane_slots(my) - groups) * my
        return np.pad(np.repeat(pair, my, axis=-1), ((0, 0),) * 4 + ((0, unused),))

    return spread(np.ones_like(amplitude)), spread(amplitude)


def dot(first, second, dims=((1,), (0,))):
    return lax.dot_general(first, second, (dims, ((), ())), preferred_element_type=F32)


def analyse_kernel(v_ref, ty_ref, tx_ref, zc_ref, o_ref, t_ref):
    groups, ny, lanes = ty_ref.shape
    half = lanes // 2
    my = o_ref.shape[-1]
    per_group, mz = zc_ref.shape[0], zc_ref.shape[1]
    mx, nx = tx_ref.shape[0] // 2, tx_ref.shape[1]
    total = None
    for i in range(groups):
        rows = v_ref[0, i * per_group:(i + 1) * per_group].reshape(per_group * nx, ny)
        part = dot(rows, ty_ref[i])
        total = part if total is None else total + part
    t_ref[...] = total.astype(BF16)
    real = [None] * mz
    imag = [None] * mz
    for j in range(per_group):
        u = dot(tx_ref[...], t_ref[j * nx:(j + 1) * nx, :])
        re = u[:mx, :half] - u[mx:, half:]
        im = u[mx:, :half] + u[:mx, half:]
        for k in range(mz):
            c = zc_ref[j, k, 0:1, :]
            s = zc_ref[j, k, 1:2, :]
            zr = re * c + im * s
            zi = im * c - re * s
            real[k] = zr if j == 0 else real[k] + zr
            imag[k] = zi if j == 0 else imag[k] + zi
    for k in range(mz):
        for part, value in enumerate((real[k], imag[k])):
            summed = value[:, :my]
            for i in range(1, groups):
                summed = summed + value[:, i * my:(i + 1) * my]
            o_ref[0, k, part] = summed


def analyse(values, ty, tx, zc, mx, my):
    c, nz, nx, ny = values.shape
    per_group, mz, lanes = zc.shape[0], zc.shape[1], zc.shape[-1]
    return pl.pallas_call(
        analyse_kernel,
        grid=(c,),
        in_specs=[
            pl.BlockSpec((1, nz, nx, ny), lambda i: (i, 0, 0, 0)),
            pl.BlockSpec(ty.shape, lambda i: (0, 0, 0)),
            pl.BlockSpec(tx.shape, lambda i: (0, 0)),
            pl.BlockSpec(zc.shape, lambda i: (0, 0, 0, 0)),
        ],
        out_specs=pl.BlockSpec((1, mz, 2, mx, my), lambda i: (i, 0, 0, 0, 0)),
        out_shape=jax.ShapeDtypeStruct((c, mz, 2, mx, my), F32),
        scratch_shapes=[pltpu.VMEM((per_group * nx, 2 * lanes), BF16)],
        compiler_params=pltpu.CompilerParams(vmem_limit_bytes=48 * 2**20),
        name="analysis",
    )(values, ty, tx, zc)


def mix_kernel(s_ref, w_ref, m_ref, wg_ref):
    mz, _, c, _ = w_ref.shape[2:]
    for k in range(mz):
        f2 = s_ref[0, 0, k, :, :c]
        g2 = s_ref[0, 0, k, :, c:]
        wk = w_ref[0, 0, k].reshape(2 * c, c)
        fm = dot(f2, wk, ((1,), (1,)))
        gm = dot(g2, wk)
        m_ref[0, 0, 0, k:k + 1, :] = fm[0:1, :c] - fm[1:2, c:]
        m_ref[0, 0, 1, k:k + 1, :] = fm[1:2, :c] + fm[0:1, c:]
        m_ref[0, 0, 2, k:k + 1, :] = gm[0:1]
        m_ref[0, 0, 3, k:k + 1, :] = gm[1:2]
        wg_ref[0, 0, k] = dot(g2, f2, ((0,), (0,))).reshape(2, c, c)


def mix(spectra, weights):
    a, b, mz, _, c, _ = weights.shape
    rows = spectra.shape[3]
    return pl.pallas_call(
        mix_kernel,
        grid=(a, b),
        in_specs=[
            pl.BlockSpec((1, 1, mz, rows, 3 * c), lambda i, j: (i, j, 0, 0, 0)),
            pl.BlockSpec((1, 1, mz, 2, c, c), lambda i, j: (i, j, 0, 0, 0, 0)),
        ],
        out_specs=[
            pl.BlockSpec((1, 1, 4, mz, c), lambda i, j: (i, j, 0, 0, 0)),
            pl.BlockSpec((1, 1, mz, 2, c, c), lambda i, j: (i, j, 0, 0, 0, 0)),
        ],
        out_shape=[
            jax.ShapeDtypeStruct((a, b, 4, mz, c), F32),
            jax.ShapeDtypeStruct((a, b, mz, 2, c, c), F32),
        ],
        compiler_params=pltpu.CompilerParams(vmem_limit_bytes=48 * 2**20),
        name="mixing",
    )(spectra, weights)


def synthesis_kernel(scale, m_ref, zc_ref, tx_ref, ty_ref, o_ref, t_ref):
    groups, lanes, ny = ty_ref.shape
    half = lanes // 2
    per_group, mz = zc_ref.shape[0], zc_ref.shape[1]
    nx = tx_ref.shape[0]
    for j in range(per_group):
        re = im = None
        for k in range(mz):
            c = zc_ref[j, k, 0:1, :]
            s = zc_ref[j, k, 1:2, :]
            mr = m_ref[0, k, 0].astype(F32)
            mi = m_ref[0, k, 1].astype(F32)
            zr = mr * c - mi * s
            zi = mi * c + mr * s
            re = zr if k == 0 else re + zr
            im = zi if k == 0 else im + zi
        re = re * scale
        im = im * scale
        upper = jnp.concatenate([re, im], 1)
        lower = jnp.concatenate([-im, re], 1)
        block = jnp.concatenate([upper, lower], 0).astype(BF16)
        t_ref[j * nx:(j + 1) * nx, :] = dot(tx_ref[...], block).astype(BF16)
    for i in range(groups):
        out = dot(t_ref[...], ty_ref[i])
        o_ref[0, i * per_group:(i + 1) * per_group] = out.astype(BF16).reshape(per_group, nx, ny)


def synthesize(spectra, zc, tx, ty, scale):
    c, mz, _, mx, lanes = spectra.shape
    per_group = zc.shape[0]
    groups, _, ny = ty.shape
    nx = tx.shape[0]
    nz = per_group * groups
    return pl.pallas_call(
        functools.partial(synthesis_kernel, scale),
        grid=(c,),
        in_specs=[
            pl.BlockSpec((1, mz, 2, mx, lanes), lambda i: (i, 0, 0, 0, 0)),
            pl.BlockSpec(zc.shape, lambda i: (0, 0, 0, 0)),
            pl.BlockSpec(tx.shape, lambda i: (0, 0)),
            pl.BlockSpec(ty.shape, lambda i: (0, 0, 0)),
        ],
        out_specs=pl.BlockSpec((1, nz, nx, ny), lambda i: (i, 0, 0, 0)),
        out_shape=jax.ShapeDtypeStruct((c, nz, nx, ny), BF16),
        scratch_shapes=[pltpu.VMEM((per_group * nx, 2 * lanes), BF16)],
        compiler_params=pltpu.CompilerParams(vmem_limit_bytes=48 * 2**20),
        name="synthesis",
    )(spectra, zc, tx, ty)


def shards(input_field, cotangent, weights):
    blk_count = lax.axis_size("blk")
    space_count = lax.axis_size("space")
    space_index = lax.axis_index("space")
    c_local, nz_local, nx, ny = input_field.shape
    px, qx, mz = weights.shape[:3]
    mx, my = px * space_count, qx * blk_count
    channels = c_local * blk_count
    nz = nz_local * space_count
    groups = lane_groups(my, nz_local)
    forward_scale = 1.0 / math.sqrt(nx * ny * nz)
    synth_scale = 1.0 / math.sqrt(mx * my * mz)
    amplitude = np.where(np.arange(mz) == 0, 1.0, 2.0).astype(np.float32)
    ty_in, ty_out = y_tables(ny, my, groups)
    tx_in, tx_out = x_tables(nx, mx)
    zc_unit, zc_amp = z_tables(nz, mz, my, space_count, groups)
    zc_unit = lax.dynamic_index_in_dim(jnp.asarray(zc_unit), space_index, 0, keepdims=False)
    zc_amp = lax.dynamic_index_in_dim(jnp.asarray(zc_amp), space_index, 0, keepdims=False)

    part_f = analyse(input_field, ty_in, tx_in, zc_unit, mx, my)
    part_g = analyse(cotangent, ty_in, tx_in, zc_unit, mx, my)
    parts = jnp.stack([part_f, part_g], 0).astype(BF16)
    parts = parts.reshape(2, c_local, mz, 2, space_count, px, blk_count, qx)
    send = parts.transpose(4, 6, 0, 2, 3, 5, 7, 1)
    send = send.reshape(space_count * blk_count, -1, 128)
    got = lax.all_to_all(send, ("space", "blk"), split_axis=0, concat_axis=0, tiled=True)
    got = got.reshape(space_count, blk_count, 2, mz, 2, px, qx, c_local)
    zsum = jnp.sum(got.astype(F32), 0)
    zsum = zsum.transpose(1, 3, 4, 5, 2, 0, 6).reshape(2, 2, px, qx, mz, channels)
    spec_f = (zsum[0] * forward_scale).astype(BF16)
    spec_g = (zsum[1] * (amplitude * np.float32(synth_scale))[:, None]).astype(BF16)
    row0 = jnp.concatenate([spec_f[0], spec_g[0], spec_g[1]], -1)
    row1 = jnp.concatenate([spec_f[1], spec_g[1], -spec_g[0]], -1)
    spectra = jnp.stack([row0, row1], 3)
    spectra = jnp.pad(spectra, ((0, 0),) * 3 + ((0, 14), (0, 0)))
    mixed, weight_grad = mix(spectra, weights)

    back = mixed.astype(BF16).reshape(px, qx, 2, 2, mz, blk_count, c_local)
    back = back.transpose(5, 2, 6, 4, 3, 0, 1).reshape(1, blk_count, -1, 128)
    back = jnp.broadcast_to(back, (space_count,) + back.shape[1:])
    back = back.reshape(space_count * blk_count, -1, 128)
    home = lax.all_to_all(back, ("space", "blk"), split_axis=0, concat_axis=0, tiled=True)
    home = home.reshape(space_count, blk_count, 2, c_local, mz, 2, px, qx)
    home = home.transpose(2, 3, 4, 5, 0, 6, 1, 7).reshape(2, c_local, mz, 2, mx, my)
    home = jnp.concatenate([home] * lane_slots(my), -1)
    spectral_out = synthesize(home[0], zc_amp, tx_out, ty_out, synth_scale)
    field_grad = synthesize(home[1], zc_unit, tx_out, ty_out, forward_scale)
    return (spectral_out, field_grad, weight_grad)


def solution(mesh):
    placed = (
        P("blk", "space", None, None),
        P("blk", "space", None, None),
        P("space", "blk", None, None, None, None),
    )
    return jax.shard_map(
        shards,
        mesh=mesh,
        in_specs=placed,
        out_specs=placed,
        check_vma=False,
    )
```

```python
import functools
import math

import jax
import jax.numpy as jnp
import numpy as np
from jax import lax
from jax.experimental import pallas as pl
from jax.experimental.pallas import tpu as pltpu
from jax.sharding import PartitionSpec as P

F32 = jnp.float32
BF16 = jnp.bfloat16


def centered_freqs(count):
    indices = np.arange(count, dtype=np.int64)
    return np.where(indices < count // 2, indices, indices - count)


def phase_pair(frequencies, positions, length):
    product = (frequencies[:, None] * positions[None, :]) % length
    angles = product.astype(np.float32) * np.float32(2.0 * math.pi / length)
    return np.cos(angles).astype(np.float32), np.sin(angles).astype(np.float32)


def rounded(table):
    return np.asarray(table, np.float32).astype(jnp.bfloat16)


def lane_slots(my):
    return max(1, 128 // my)


def lane_groups(my, local):
    return math.gcd(lane_slots(my), local)


def y_tables(ny, my, groups):
    cosines, sines = phase_pair(centered_freqs(my), np.arange(ny), ny)
    half = lane_slots(my) * my
    forward = np.zeros((groups, ny, 2 * half), np.float32)
    for i in range(groups):
        forward[i, :, i * my:(i + 1) * my] = cosines.T
        forward[i, :, half + i * my:half + (i + 1) * my] = -sines.T
    return rounded(forward), rounded(np.swapaxes(forward, 1, 2))


def x_tables(nx, mx):
    cosines, sines = phase_pair(centered_freqs(mx), np.arange(nx), nx)
    forward = np.concatenate([cosines, -sines], 0)
    backward = np.concatenate([cosines, sines], 0).T
    return rounded(forward), rounded(backward)


def z_tables(nz, mz, my, space_count, groups):
    cosines, sines = phase_pair(np.arange(mz), np.arange(nz), nz)
    local = nz // space_count
    per_group = local // groups
    amplitude = np.where(np.arange(mz) == 0, 1.0, 2.0).astype(np.float32)[:, None]

    def spread(weight):
        pair = np.stack([rounded(cosines * weight), rounded(sines * weight)], 1).astype(np.float32)
        pair = pair.reshape(mz, 2, space_count, groups, per_group)
        pair = pair.transpose(2, 4, 0, 1, 3)
        unused = (lane_slots(my) - groups) * my
        return np.pad(np.repeat(pair, my, axis=-1), ((0, 0),) * 4 + ((0, unused),))

    return spread(np.ones_like(amplitude)), spread(amplitude)


def dot(first, second, dims=((1,), (0,))):
    return lax.dot_general(first, second, (dims, ((), ())), preferred_element_type=F32)


def every(start, count, stride):
    return pl.ds(start, count) if stride == 1 else pl.ds(start, count, stride=stride)


def analyse_kernel(f_ref, g_ref, ty_ref, tx_ref, zc_ref, o_ref, t_ref, zs_ref):
    groups, ny, lanes = ty_ref.shape
    half = lanes // 2
    space, blk, _, qx, width = o_ref.shape
    my = blk * qx
    per_group, mz = zc_ref.shape[0], zc_ref.shape[1]
    mx, nx = tx_ref.shape[0] // 2, tx_ref.shape[1]
    for h, v_ref in enumerate((f_ref, g_ref)):
        total = None
        for i in range(groups):
            rows = v_ref[0, i * per_group:(i + 1) * per_group].reshape(per_group * nx, ny)
            part = dot(rows, ty_ref[i])
            total = part if total is None else total + part
        t_ref[h] = total.astype(BF16)
        real = [None] * mz
        imag = [None] * mz
        for j in range(per_group):
            u = dot(tx_ref[...], t_ref[h, j * nx:(j + 1) * nx, :])
            re = u[:mx, :half] - u[mx:, half:]
            im = u[mx:, :half] + u[:mx, half:]
            for k in range(mz):
                c = zc_ref[j, k, 0:1, :]
                s = zc_ref[j, k, 1:2, :]
                zr = re * c + im * s
                zi = im * c - re * s
                real[k] = zr if j == 0 else real[k] + zr
                imag[k] = zi if j == 0 else imag[k] + zi
        for k in range(mz):
            zs_ref[every(4 * k + 2 * h, mx, 4 * mz), :] = real[k]
            zs_ref[every(4 * k + 2 * h + 1, mx, 4 * mz), :] = imag[k]
    flipped = zs_ref[...].T
    summed = flipped[:my]
    for i in range(1, half // my):
        summed = summed + flipped[i * my:(i + 1) * my]
    for s in range(space):
        for b in range(blk):
            o_ref[s, b, 0] = summed[b * qx:(b + 1) * qx, s * width:(s + 1) * width]


def analyse(first, second, ty, tx, zc, sent):
    c, nz, nx, ny = first.shape
    per_group, mz, half = zc.shape[0], zc.shape[1], zc.shape[-1]
    mx = tx.shape[0] // 2
    space, blk, _, qx, width = sent
    return pl.pallas_call(
        analyse_kernel,
        grid=(c,),
        in_specs=[
            pl.BlockSpec((1, nz, nx, ny), lambda i: (i, 0, 0, 0)),
            pl.BlockSpec((1, nz, nx, ny), lambda i: (i, 0, 0, 0)),
            pl.BlockSpec(ty.shape, lambda i: (0, 0, 0)),
            pl.BlockSpec(tx.shape, lambda i: (0, 0)),
            pl.BlockSpec(zc.shape, lambda i: (0, 0, 0, 0)),
        ],
        out_specs=pl.BlockSpec((space, blk, 1, qx, width), lambda i: (0, 0, i, 0, 0)),
        out_shape=jax.ShapeDtypeStruct(sent, F32),
        scratch_shapes=[
            pltpu.VMEM((2, per_group * nx, 2 * half), BF16),
            pltpu.VMEM((mx * mz * 4, half), F32),
        ],
        compiler_params=pltpu.CompilerParams(vmem_limit_bytes=48 * 2**20),
        name="analysis",
    )(first, second, ty, tx, zc)


def mix_kernel(s_ref, scale_ref, w_ref, o_ref, wg_ref, sum_ref, in_ref, out_ref):
    mz, _, c, _ = w_ref.shape[2:]
    qx = in_ref.shape[0]
    rows = 4 * mz
    a, j = pl.program_id(0), pl.program_id(1)

    @pl.when((a == 0) & (j == 0))
    def _():
        total = s_ref[0].astype(F32)
        for s in range(1, s_ref.shape[0]):
            total = total + s_ref[s].astype(F32)
        sum_ref[...] = total
        for i in range(qx):
            in_ref[i] = sum_ref[every(i, c, qx), :].T * scale_ref[...]

    start = pl.multiple_of(a * rows, 8)
    x = in_ref[j, pl.ds(start, rows), :]
    mixed = []
    for k in range(mz):
        fr, fi, gr, gi = (x[4 * k + i:4 * k + i + 1] for i in range(4))
        row0 = jnp.concatenate([fr, gr, gi], 1)
        row1 = jnp.concatenate([fi, gi, -gr], 1)
        both = jnp.concatenate([row0, row1, jnp.zeros((14, 3 * c), F32)], 0).astype(BF16)
        f2 = both[:, :c]
        g2 = both[:, c:]
        wk = w_ref[0, 0, k].reshape(2 * c, c)
        fm = dot(f2, wk, ((1,), (1,)))
        gm = dot(g2, wk)
        mixed += [fm[0:1, :c] - fm[1:2, c:], fm[1:2, :c] + fm[0:1, c:], gm[0:2]]
        wg_ref[0, 0, k] = dot(g2, f2, ((0,), (0,))).reshape(2, c, c)
    out_ref[j, pl.ds(start, rows), :] = jnp.concatenate(mixed, 0)

    @pl.when((a == pl.num_programs(0) - 1) & (j == pl.num_programs(1) - 1))
    def _():
        for i in range(qx):
            o_ref[every(i, c, qx), :] = out_ref[i].T


def mix(spectra, scales, weights):
    a, b, mz, _, c, _ = weights.shape
    rows, width = spectra.shape[1:]
    return pl.pallas_call(
        mix_kernel,
        grid=(a, b),
        in_specs=[
            pl.BlockSpec(spectra.shape, lambda i, j: (0, 0, 0)),
            pl.BlockSpec(scales.shape, lambda i, j: (0, 0)),
            pl.BlockSpec((1, 1, mz, 2, c, c), lambda i, j: (i, j, 0, 0, 0, 0)),
        ],
        out_specs=[
            pl.BlockSpec((rows, width), lambda i, j: (0, 0)),
            pl.BlockSpec((1, 1, mz, 2, c, c), lambda i, j: (i, j, 0, 0, 0, 0)),
        ],
        out_shape=[
            jax.ShapeDtypeStruct((rows, width), F32),
            jax.ShapeDtypeStruct((a, b, mz, 2, c, c), F32),
        ],
        scratch_shapes=[
            pltpu.VMEM((rows, width), F32),
            pltpu.VMEM((b, width, c), F32),
            pltpu.VMEM((b, width, c), F32),
        ],
        compiler_params=pltpu.CompilerParams(vmem_limit_bytes=48 * 2**20),
        name="mixing",
    )(spectra, scales, weights)


def synthesis_kernel(scales, m_ref, za_ref, zu_ref, tx_ref, ty_ref, y_ref, u_ref, t_ref, zs_ref):
    groups, lanes, ny = ty_ref.shape
    half = lanes // 2
    space, blk, _, qx, width = m_ref.shape
    my = blk * qx
    per_group, mz = za_ref.shape[0], za_ref.shape[1]
    nx, mx = tx_ref.shape[0], tx_ref.shape[1] // 2
    columns = []
    for s in range(space):
        columns.append(jnp.concatenate([m_ref[s, b, 0] for b in range(blk)], 0))
    spectrum = jnp.concatenate(columns, 1)
    zs_ref[...] = jnp.concatenate([spectrum] * (half // my), 0).T
    for h, (zc_ref, o_ref) in enumerate(((za_ref, y_ref), (zu_ref, u_ref))):
        real = [zs_ref[every(4 * k + 2 * h, mx, 4 * mz), :] for k in range(mz)]
        imag = [zs_ref[every(4 * k + 2 * h + 1, mx, 4 * mz), :] for k in range(mz)]
        for j in range(per_group):
            re = im = None
            for k in range(mz):
                c = zc_ref[j, k, 0:1, :]
                s = zc_ref[j, k, 1:2, :]
                zr = real[k] * c - imag[k] * s
                zi = imag[k] * c + real[k] * s
                re = zr if k == 0 else re + zr
                im = zi if k == 0 else im + zi
            re = re * scales[h]
            im = im * scales[h]
            upper = jnp.concatenate([re, im], 1)
            lower = jnp.concatenate([-im, re], 1)
            block = jnp.concatenate([upper, lower], 0).astype(BF16)
            t_ref[h, j * nx:(j + 1) * nx, :] = dot(tx_ref[...], block).astype(BF16)
        for i in range(groups):
            out = dot(t_ref[h], ty_ref[i]).astype(BF16)
            o_ref[0, i * per_group:(i + 1) * per_group] = out.reshape(per_group, nx, ny)


def synthesize(spectra, za, zu, tx, ty, scales):
    space, blk, c, qx, width = spectra.shape
    per_group, mz, half = za.shape[0], za.shape[1], za.shape[-1]
    groups, _, ny = ty.shape
    nx, mx = tx.shape[0], tx.shape[1] // 2
    nz = per_group * groups
    field = pl.BlockSpec((1, nz, nx, ny), lambda i: (i, 0, 0, 0))
    return pl.pallas_call(
        functools.partial(synthesis_kernel, scales),
        grid=(c,),
        in_specs=[
            pl.BlockSpec((space, blk, 1, qx, width), lambda i: (0, 0, i, 0, 0)),
            pl.BlockSpec(za.shape, lambda i: (0, 0, 0, 0)),
            pl.BlockSpec(zu.shape, lambda i: (0, 0, 0, 0)),
            pl.BlockSpec(tx.shape, lambda i: (0, 0)),
            pl.BlockSpec(ty.shape, lambda i: (0, 0, 0)),
        ],
        out_specs=[field, field],
        out_shape=[jax.ShapeDtypeStruct((c, nz, nx, ny), BF16)] * 2,
        scratch_shapes=[
            pltpu.VMEM((2, per_group * nx, 2 * half), BF16),
            pltpu.VMEM((mx * mz * 4, half), F32),
        ],
        compiler_params=pltpu.CompilerParams(vmem_limit_bytes=48 * 2**20),
        name="synthesis",
    )(spectra, za, zu, tx, ty)


def shards(input_field, cotangent, weights):
    blk_count = lax.axis_size("blk")
    space_count = lax.axis_size("space")
    space_index = lax.axis_index("space")
    c_local, nz_local, nx, ny = input_field.shape
    px, qx, mz = weights.shape[:3]
    mx, my = px * space_count, qx * blk_count
    channels = c_local * blk_count
    nz = nz_local * space_count
    groups = lane_groups(my, nz_local)
    devices = space_count * blk_count
    forward_scale = 1.0 / math.sqrt(nx * ny * nz)
    synth_scale = 1.0 / math.sqrt(mx * my * mz)
    amplitude = np.where(np.arange(mz) == 0, 1.0, 2.0).astype(np.float32)
    ty_in, ty_out = y_tables(ny, my, groups)
    tx_in, tx_out = x_tables(nx, mx)
    zc_unit, zc_amp = z_tables(nz, mz, my, space_count, groups)
    zc_unit = lax.dynamic_index_in_dim(jnp.asarray(zc_unit), space_index, 0, keepdims=False)
    zc_amp = lax.dynamic_index_in_dim(jnp.asarray(zc_amp), space_index, 0, keepdims=False)
    width = px * mz * 4
    sent = (space_count, blk_count, c_local, qx, width)
    scales = np.empty((px, mz, 2, 2, channels), np.float32)
    scales[:, :, 0] = np.float32(forward_scale)
    scales[:, :, 1] = (amplitude * np.float32(synth_scale))[None, :, None, None]
    scales = scales.reshape(width, channels)

    def exchange(send):
        return lax.all_to_all(send, ("space", "blk"), split_axis=0, concat_axis=0, tiled=True)

    parts = analyse(input_field, cotangent, ty_in, tx_in, zc_unit, sent)
    got = exchange(parts.reshape(devices, -1, 128).astype(BF16))
    got = got.reshape(space_count, channels * qx, width)
    mixed, weight_grad = mix(got, scales, weights)

    back = mixed.reshape(1, blk_count, -1, 128).astype(BF16)
    back = jnp.broadcast_to(back, (space_count,) + back.shape[1:])
    home = exchange(back.reshape(devices, -1, 128))
    home = home.astype(F32).reshape(sent)
    spectral_out, field_grad = synthesize(
        home, zc_amp, zc_unit, tx_out, ty_out, (synth_scale, forward_scale)
    )
    return (spectral_out, field_grad, weight_grad)


def solution(mesh):
    placed = (
        P("blk", "space", None, None),
        P("blk", "space", None, None),
        P("space", "blk", None, None, None, None),
    )
    return jax.shard_map(
        shards,
        mesh=mesh,
        in_specs=placed,
        out_specs=placed,
        check_vma=False,
    )
```

```python
import functools
import math

import jax
import jax.numpy as jnp
import numpy as np
from jax import lax
from jax.experimental import pallas as pl
from jax.experimental.pallas import tpu as pltpu
from jax.sharding import PartitionSpec as P

F32 = jnp.float32
BF16 = jnp.bfloat16


def centered_freqs(count):
    indices = np.arange(count, dtype=np.int64)
    return np.where(indices < count // 2, indices, indices - count)


def phase_pair(frequencies, positions, length):
    product = (frequencies[:, None] * positions[None, :]) % length
    angles = product.astype(np.float32) * np.float32(2.0 * math.pi / length)
    return np.cos(angles).astype(np.float32), np.sin(angles).astype(np.float32)


def rounded(table):
    return np.asarray(table, np.float32).astype(jnp.bfloat16)


def lane_slots(my):
    return max(1, 128 // my)


def lane_groups(my, local):
    return math.gcd(lane_slots(my), local)


def y_tables(ny, my, groups):
    cosines, sines = phase_pair(centered_freqs(my), np.arange(ny), ny)
    half = lane_slots(my) * my
    forward = np.zeros((groups, ny, 2 * half), np.float32)
    for i in range(groups):
        forward[i, :, i * my:(i + 1) * my] = cosines.T
        forward[i, :, half + i * my:half + (i + 1) * my] = -sines.T
    return rounded(forward), rounded(np.swapaxes(forward, 1, 2))


def x_tables(nx, mx):
    cosines, sines = phase_pair(centered_freqs(mx), np.arange(nx), nx)
    forward = np.concatenate([cosines, -sines], 0)
    backward = np.concatenate([cosines, sines], 0).T
    return rounded(forward), rounded(backward)


def z_tables(nz, mz, my, space_count, groups):
    cosines, sines = phase_pair(np.arange(mz), np.arange(nz), nz)
    local = nz // space_count
    per_group = local // groups
    amplitude = np.where(np.arange(mz) == 0, 1.0, 2.0).astype(np.float32)[:, None]

    def spread(weight):
        pair = np.stack([rounded(cosines * weight), rounded(sines * weight)], 1).astype(np.float32)
        pair = pair.reshape(mz, 2, space_count, groups, per_group)
        pair = pair.transpose(2, 4, 0, 1, 3)
        unused = (lane_slots(my) - groups) * my
        return np.pad(np.repeat(pair, my, axis=-1), ((0, 0),) * 4 + ((0, unused),))

    return spread(np.ones_like(amplitude)), spread(amplitude)


def dot(first, second, dims=((1,), (0,))):
    return lax.dot_general(first, second, (dims, ((), ())), preferred_element_type=F32)


def estimate(flops, moved):
    return pl.CostEstimate(flops=int(flops), bytes_accessed=int(moved), transcendentals=0)


def every(start, count, stride):
    return pl.ds(start, count) if stride == 1 else pl.ds(start, count, stride=stride)


def analyse_kernel(f_ref, g_ref, ty_ref, tx_ref, zc_ref, o_ref, t_ref, zs_ref):
    groups, ny, lanes = ty_ref.shape
    half = lanes // 2
    space, blk, _, qx, width = o_ref.shape
    my = blk * qx
    per_group, mz = zc_ref.shape[0], zc_ref.shape[1]
    mx, nx = tx_ref.shape[0] // 2, tx_ref.shape[1]
    for h, v_ref in enumerate((f_ref, g_ref)):
        total = None
        for i in range(groups):
            rows = v_ref[0, i * per_group:(i + 1) * per_group].reshape(per_group * nx, ny)
            part = dot(rows, ty_ref[i])
            total = part if total is None else total + part
        t_ref[h] = total.astype(BF16)
        real = [None] * mz
        imag = [None] * mz
        for j in range(per_group):
            u = dot(tx_ref[...], t_ref[h, j * nx:(j + 1) * nx, :])
            re = u[:mx, :half] - u[mx:, half:]
            im = u[mx:, :half] + u[:mx, half:]
            for k in range(mz):
                c = zc_ref[j, k, 0:1, :]
                s = zc_ref[j, k, 1:2, :]
                zr = re * c + im * s
                zi = im * c - re * s
                real[k] = zr if j == 0 else real[k] + zr
                imag[k] = zi if j == 0 else imag[k] + zi
        for k in range(mz):
            zs_ref[every(4 * k + 2 * h, mx, 4 * mz), :] = real[k]
            zs_ref[every(4 * k + 2 * h + 1, mx, 4 * mz), :] = imag[k]
    flipped = zs_ref[...].T
    summed = flipped[:my]
    for i in range(1, half // my):
        summed = summed + flipped[i * my:(i + 1) * my]
    for s in range(space):
        for b in range(blk):
            o_ref[s, b, 0] = summed[b * qx:(b + 1) * qx, s * width:(s + 1) * width]


def analyse(first, second, ty, tx, zc, sent, offset):
    nz, nx, ny = first.shape[1:]
    per_group, mz, half = zc.shape[0], zc.shape[1], zc.shape[-1]
    mx = tx.shape[0] // 2
    space, blk, c, qx, width = sent
    return pl.pallas_call(
        analyse_kernel,
        grid=(c,),
        in_specs=[
            pl.BlockSpec((1, nz, nx, ny), lambda i: (i + offset, 0, 0, 0)),
            pl.BlockSpec((1, nz, nx, ny), lambda i: (i + offset, 0, 0, 0)),
            pl.BlockSpec(ty.shape, lambda i: (0, 0, 0)),
            pl.BlockSpec(tx.shape, lambda i: (0, 0)),
            pl.BlockSpec(zc.shape, lambda i: (0, 0, 0, 0)),
        ],
        out_specs=pl.BlockSpec((space, blk, 1, qx, width), lambda i: (0, 0, i, 0, 0)),
        out_shape=jax.ShapeDtypeStruct(sent, F32),
        scratch_shapes=[
            pltpu.VMEM((2, per_group * nx, 2 * half), BF16),
            pltpu.VMEM((mx * mz * 4, half), F32),
        ],
        compiler_params=pltpu.CompilerParams(vmem_limit_bytes=48 * 2**20),
        cost_estimate=estimate(2 * c * nz * nx * ny * 2 * 256, 4 * c * nz * nx * ny),
        name="analysis",
    )(first, second, ty, tx, zc)


def pair_rows(x, k, c):
    fr, fi, gr, gi = (x[4 * k + i:4 * k + i + 1] for i in range(4))
    row0 = jnp.concatenate([fr, gr, gi], 1)
    row1 = jnp.concatenate([fi, gi, -gr], 1)
    both = jnp.concatenate([row0, row1, jnp.zeros((14, 3 * c), F32)], 0).astype(BF16)
    return both[:, :c], both[:, c:]


def mix_kernel(parts, *refs):
    s_refs, (scale_ref, w_ref) = refs[:parts], refs[parts:parts + 2]
    o_refs, (in_ref, sum_ref, out_ref) = refs[parts + 2:-3], refs[-3:]
    mz, _, c, _ = w_ref.shape[2:]
    qx = in_ref.shape[0]
    blk, depth, width = s_refs[0].shape[1:]
    rows = 4 * mz
    a, j = pl.program_id(0), pl.program_id(1)

    @pl.when((a == 0) & (j == 0))
    def _():
        totals = []
        for s_ref in s_refs:
            total = s_ref[0].astype(F32)
            for s in range(1, s_ref.shape[0]):
                total = total + s_ref[s].astype(F32)
            totals.append(total)
        sum_ref[...] = jnp.concatenate(totals, 1).reshape(c * qx, width)
        for i in range(qx):
            in_ref[i] = sum_ref[every(i, c, qx), :].T * scale_ref[...]

    start = pl.multiple_of(a * rows, 8)
    x = in_ref[j, pl.ds(start, rows), :]
    mixed = []
    for k in range(mz):
        f2, g2 = pair_rows(x, k, c)
        wk = w_ref[0, 0, k].reshape(2 * c, c)
        fm = dot(f2, wk, ((1,), (1,)))
        gm = dot(g2, wk)
        mixed += [fm[0:1, :c] - fm[1:2, c:], fm[1:2, :c] + fm[0:1, c:], gm[0:2]]
    out_ref[j, pl.ds(start, rows), :] = jnp.concatenate(mixed, 0)

    @pl.when((a == pl.num_programs(0) - 1) & (j == pl.num_programs(1) - 1))
    def _():
        for i in range(qx):
            sum_ref[every(i, c, qx), :] = out_ref[i].T
        back = sum_ref[...].reshape(blk, parts * depth, width)
        for part, o_ref in enumerate(o_refs):
            piece = back[:, part * depth:(part + 1) * depth].astype(BF16)
            for s in range(o_ref.shape[0]):
                o_ref[s] = piece


def mix(spectra, scales, weights):
    a, b, mz, _, c, _ = weights.shape
    sent = spectra[0].shape
    width = sent[-1]
    whole = pl.BlockSpec(sent, lambda i, j: (0, 0, 0, 0))
    return pl.pallas_call(
        functools.partial(mix_kernel, len(spectra)),
        grid=(a, b),
        in_specs=[whole] * len(spectra) + [
            pl.BlockSpec(scales.shape, lambda i, j: (0, 0)),
            pl.BlockSpec((1, 1, mz, 2, c, c), lambda i, j: (i, j, 0, 0, 0, 0)),
        ],
        out_specs=[whole] * len(spectra) + [pl.BlockSpec((b, width, c), lambda i, j: (0, 0, 0))],
        out_shape=[jax.ShapeDtypeStruct(sent, BF16)] * len(spectra)
        + [jax.ShapeDtypeStruct((b, width, c), F32)],
        scratch_shapes=[
            pltpu.VMEM((c * b, width), F32),
            pltpu.VMEM((b, width, c), F32),
        ],
        compiler_params=pltpu.CompilerParams(vmem_limit_bytes=48 * 2**20),
        cost_estimate=estimate(a * b * mz * c * c * 128, 2 * weights.size),
        name="mixing",
    )(*spectra, scales, weights)


def outer_kernel(in_ref, wg_ref):
    mz, _, c, _ = wg_ref.shape[2:]
    rows = 4 * mz
    start = pl.multiple_of(pl.program_id(0) * rows, 8)
    x = in_ref[pl.program_id(1), pl.ds(start, rows), :]
    for k in range(mz):
        f2, g2 = pair_rows(x, k, c)
        wg_ref[0, 0, k] = dot(g2, f2, ((0,), (0,))).reshape(2, c, c)


def outer(spectra, shape):
    a, b, mz, _, c, _ = shape
    return pl.pallas_call(
        outer_kernel,
        grid=(a, b),
        in_specs=[pl.BlockSpec(spectra.shape, lambda i, j: (0, 0, 0))],
        out_specs=pl.BlockSpec((1, 1, mz, 2, c, c), lambda i, j: (i, j, 0, 0, 0, 0)),
        out_shape=jax.ShapeDtypeStruct(shape, F32),
        compiler_params=pltpu.CompilerParams(vmem_limit_bytes=48 * 2**20),
        cost_estimate=estimate(a * b * mz * c * c * 64, 8 * a * b * mz * c * c),
        name="weight_grad",
    )(spectra)


def synthesis_kernel(scales, m_ref, za_ref, zu_ref, tx_ref, ty_ref, *refs):
    y_ref, u_ref, t_ref, zs_ref = refs[-4:]
    groups, lanes, ny = ty_ref.shape
    half = lanes // 2
    space, blk, _, qx, width = m_ref.shape
    my = blk * qx
    per_group, mz = za_ref.shape[0], za_ref.shape[1]
    nx, mx = tx_ref.shape[0], tx_ref.shape[1] // 2
    columns = []
    for s in range(space):
        columns.append(jnp.concatenate([m_ref[s, b, 0] for b in range(blk)], 0))
    spectrum = jnp.concatenate(columns, 1)
    zs_ref[...] = jnp.concatenate([spectrum] * (half // my), 0).T
    for h, (zc_ref, o_ref) in enumerate(((za_ref, y_ref), (zu_ref, u_ref))):
        real = [zs_ref[every(4 * k + 2 * h, mx, 4 * mz), :] for k in range(mz)]
        imag = [zs_ref[every(4 * k + 2 * h + 1, mx, 4 * mz), :] for k in range(mz)]
        for j in range(per_group):
            re = im = None
            for k in range(mz):
                c = zc_ref[j, k, 0:1, :]
                s = zc_ref[j, k, 1:2, :]
                zr = real[k] * c - imag[k] * s
                zi = imag[k] * c + real[k] * s
                re = zr if k == 0 else re + zr
                im = zi if k == 0 else im + zi
            re = re * scales[h]
            im = im * scales[h]
            upper = jnp.concatenate([re, im], 1)
            lower = jnp.concatenate([-im, re], 1)
            block = jnp.concatenate([upper, lower], 0).astype(BF16)
            t_ref[h, j * nx:(j + 1) * nx, :] = dot(tx_ref[...], block).astype(BF16)
        for i in range(groups):
            out = dot(t_ref[h], ty_ref[i]).astype(BF16)
            o_ref[0, i * per_group:(i + 1) * per_group] = out.reshape(per_group, nx, ny)


def synthesize(spectra, za, zu, tx, ty, scales, channels, offset, earlier):
    space, blk, c, qx, width = spectra.shape
    per_group, mz, half = za.shape[0], za.shape[1], za.shape[-1]
    groups, _, ny = ty.shape
    nx, mx = tx.shape[0], tx.shape[1] // 2
    nz = per_group * groups
    field = pl.BlockSpec((1, nz, nx, ny), lambda i: (i + offset, 0, 0, 0))
    return pl.pallas_call(
        functools.partial(synthesis_kernel, scales),
        grid=(c,),
        in_specs=[
            pl.BlockSpec((space, blk, 1, qx, width), lambda i: (0, 0, i, 0, 0)),
            pl.BlockSpec(za.shape, lambda i: (0, 0, 0, 0)),
            pl.BlockSpec(zu.shape, lambda i: (0, 0, 0, 0)),
            pl.BlockSpec(tx.shape, lambda i: (0, 0)),
            pl.BlockSpec(ty.shape, lambda i: (0, 0, 0)),
        ] + [pl.BlockSpec(memory_space=pl.ANY)] * len(earlier),
        out_specs=[field, field],
        out_shape=[jax.ShapeDtypeStruct((channels, nz, nx, ny), BF16)] * 2,
        input_output_aliases={5 + i: i for i in range(len(earlier))},
        scratch_shapes=[
            pltpu.VMEM((2, per_group * nx, 2 * half), BF16),
            pltpu.VMEM((mx * mz * 4, half), F32),
        ],
        compiler_params=pltpu.CompilerParams(vmem_limit_bytes=48 * 2**20),
        cost_estimate=estimate(2 * c * nz * nx * ny * 2 * 256, 4 * c * nz * nx * ny),
        name="synthesis",
    )(spectra, za, zu, tx, ty, *earlier)


def shards(input_field, cotangent, weights):
    blk_count = lax.axis_size("blk")
    space_count = lax.axis_size("space")
    space_index = lax.axis_index("space")
    c_local, nz_local, nx, ny = input_field.shape
    px, qx, mz = weights.shape[:3]
    mx, my = px * space_count, qx * blk_count
    channels = c_local * blk_count
    nz = nz_local * space_count
    groups = lane_groups(my, nz_local)
    devices = space_count * blk_count
    forward_scale = 1.0 / math.sqrt(nx * ny * nz)
    synth_scale = 1.0 / math.sqrt(mx * my * mz)
    amplitude = np.where(np.arange(mz) == 0, 1.0, 2.0).astype(np.float32)
    ty_in, ty_out = y_tables(ny, my, groups)
    tx_in, tx_out = x_tables(nx, mx)
    zc_unit, zc_amp = z_tables(nz, mz, my, space_count, groups)
    zc_unit = lax.dynamic_index_in_dim(jnp.asarray(zc_unit), space_index, 0, keepdims=False)
    zc_amp = lax.dynamic_index_in_dim(jnp.asarray(zc_amp), space_index, 0, keepdims=False)
    width = px * mz * 4
    halves = 2 if c_local % 2 == 0 else 1
    c_part = c_local // halves
    sent = (space_count, blk_count, c_part, qx, width)
    scales = np.empty((px, mz, 2, 2, channels), np.float32)
    scales[:, :, 0] = np.float32(forward_scale)
    scales[:, :, 1] = (amplitude * np.float32(synth_scale))[None, :, None, None]
    scales = scales.reshape(width, channels)

    def exchange(send):
        return lax.all_to_all(send, ("space", "blk"), split_axis=0, concat_axis=0, tiled=True)

    got = []
    for part in range(halves):
        own = analyse(input_field, cotangent, ty_in, tx_in, zc_unit, sent, part * c_part)
        moved = exchange(own.reshape(devices, c_part * qx, width).astype(BF16))
        got.append(moved.reshape(space_count, blk_count, c_part * qx, width))
    *back, spectra = mix(got, scales, weights)
    weight_grad = outer(spectra, weights.shape)

    outs = ()
    for part in range(halves):
        home = exchange(back[part].reshape(devices, c_part * qx, width))
        home = home.astype(F32).reshape(sent)
        outs = synthesize(
            home, zc_amp, zc_unit, tx_out, ty_out, (synth_scale, forward_scale),
            c_local, part * c_part, outs,
        )
    return (outs[0], outs[1], weight_grad)


def solution(mesh):
    placed = (
        P("blk", "space", None, None),
        P("blk", "space", None, None),
        P("space", "blk", None, None, None, None),
    )
    return jax.shard_map(
        shards,
        mesh=mesh,
        in_specs=placed,
        out_specs=placed,
        check_vma=False,
    )
```

```python
import functools
import math

import jax
import jax.numpy as jnp
import numpy as np
from jax import lax
from jax.experimental import pallas as pl
from jax.experimental.pallas import tpu as pltpu
from jax.sharding import PartitionSpec as P

F32 = jnp.float32
BF16 = jnp.bfloat16


def centered_freqs(count):
    indices = np.arange(count, dtype=np.int64)
    return np.where(indices < count // 2, indices, indices - count)


def phase_pair(frequencies, positions, length):
    product = (frequencies[:, None] * positions[None, :]) % length
    angles = product.astype(np.float32) * np.float32(2.0 * math.pi / length)
    return np.cos(angles).astype(np.float32), np.sin(angles).astype(np.float32)


def rounded(table):
    return np.asarray(table, np.float32).astype(jnp.bfloat16)


def lane_slots(my):
    return max(1, 128 // my)


def lane_groups(my, local):
    return math.gcd(lane_slots(my), local)


def y_tables(ny, my, groups):
    cosines, sines = phase_pair(centered_freqs(my), np.arange(ny), ny)
    half = lane_slots(my) * my
    forward = np.zeros((groups, ny, 2 * half), np.float32)
    for i in range(groups):
        forward[i, :, i * my:(i + 1) * my] = cosines.T
        forward[i, :, half + i * my:half + (i + 1) * my] = -sines.T
    return rounded(forward), rounded(np.swapaxes(forward, 1, 2))


def x_tables(nx, mx):
    cosines, sines = phase_pair(centered_freqs(mx), np.arange(nx), nx)
    forward = np.concatenate([cosines, -sines], 0)
    backward = np.concatenate([cosines, sines], 0).T
    return rounded(forward), rounded(backward)


def z_tables(nz, mz, my, space_count, groups):
    cosines, sines = phase_pair(np.arange(mz), np.arange(nz), nz)
    local = nz // space_count
    per_group = local // groups
    amplitude = np.where(np.arange(mz) == 0, 1.0, 2.0).astype(np.float32)[:, None]

    def spread(weight):
        pair = np.stack([rounded(cosines * weight), rounded(sines * weight)], 1).astype(np.float32)
        pair = pair.reshape(mz, 2, space_count, groups, per_group)
        pair = pair.transpose(2, 4, 0, 1, 3)
        unused = (lane_slots(my) - groups) * my
        return np.pad(np.repeat(pair, my, axis=-1), ((0, 0),) * 4 + ((0, unused),))

    return spread(np.ones_like(amplitude)), spread(amplitude)


def dot(first, second, dims=((1,), (0,))):
    return lax.dot_general(first, second, (dims, ((), ())), preferred_element_type=F32)


def estimate(flops, moved):
    return pl.CostEstimate(flops=int(flops), bytes_accessed=int(moved), transcendentals=0)


def every(start, count, stride):
    return pl.ds(start, count) if stride == 1 else pl.ds(start, count, stride=stride)


def analyse_kernel(f_ref, g_ref, ty_ref, tx_ref, zc_ref, o_ref, t_ref, zs_ref):
    groups, ny, lanes = ty_ref.shape
    half = lanes // 2
    space, blk, _, qx, width = o_ref.shape
    my = blk * qx
    per_group, mz = zc_ref.shape[0], zc_ref.shape[1]
    mx, nx = tx_ref.shape[0] // 2, tx_ref.shape[1]
    for h, v_ref in enumerate((f_ref, g_ref)):
        total = None
        for i in range(groups):
            rows = v_ref[0, i * per_group:(i + 1) * per_group].reshape(per_group * nx, ny)
            part = dot(rows, ty_ref[i])
            total = part if total is None else total + part
        t_ref[h] = total.astype(BF16)
        real = [None] * mz
        imag = [None] * mz
        for j in range(per_group):
            u = dot(tx_ref[...], t_ref[h, j * nx:(j + 1) * nx, :])
            re = u[:mx, :half] - u[mx:, half:]
            im = u[mx:, :half] + u[:mx, half:]
            for k in range(mz):
                c = zc_ref[j, k, 0:1, :]
                s = zc_ref[j, k, 1:2, :]
                zr = re * c + im * s
                zi = im * c - re * s
                real[k] = zr if j == 0 else real[k] + zr
                imag[k] = zi if j == 0 else imag[k] + zi
        for k in range(mz):
            zs_ref[every(4 * k + 2 * h, mx, 4 * mz), :] = real[k]
            zs_ref[every(4 * k + 2 * h + 1, mx, 4 * mz), :] = imag[k]
    flipped = zs_ref[...].T
    summed = flipped[:my]
    for i in range(1, half // my):
        summed = summed + flipped[i * my:(i + 1) * my]
    for s in range(space):
        for b in range(blk):
            o_ref[s, b, 0] = summed[b * qx:(b + 1) * qx, s * width:(s + 1) * width]


def analyse(first, second, ty, tx, zc, sent, offset):
    nz, nx, ny = first.shape[1:]
    per_group, mz, half = zc.shape[0], zc.shape[1], zc.shape[-1]
    mx = tx.shape[0] // 2
    space, blk, c, qx, width = sent
    return pl.pallas_call(
        analyse_kernel,
        grid=(c,),
        in_specs=[
            pl.BlockSpec((1, nz, nx, ny), lambda i: (i + offset, 0, 0, 0)),
            pl.BlockSpec((1, nz, nx, ny), lambda i: (i + offset, 0, 0, 0)),
            pl.BlockSpec(ty.shape, lambda i: (0, 0, 0)),
            pl.BlockSpec(tx.shape, lambda i: (0, 0)),
            pl.BlockSpec(zc.shape, lambda i: (0, 0, 0, 0)),
        ],
        out_specs=pl.BlockSpec((space, blk, 1, qx, width), lambda i: (0, 0, i, 0, 0)),
        out_shape=jax.ShapeDtypeStruct(sent, F32),
        scratch_shapes=[
            pltpu.VMEM((2, per_group * nx, 2 * half), BF16),
            pltpu.VMEM((mx * mz * 4, half), F32),
        ],
        compiler_params=pltpu.CompilerParams(vmem_limit_bytes=48 * 2**20),
        cost_estimate=estimate(2 * c * nz * nx * ny * 2 * 256, 4 * c * nz * nx * ny),
        name="analysis",
    )(first, second, ty, tx, zc)


def pair_rows(x, k, c):
    fr, fi, gr, gi = (x[4 * k + i:4 * k + i + 1] for i in range(4))
    row0 = jnp.concatenate([fr, gr, gi], 1)
    row1 = jnp.concatenate([fi, gi, -gr], 1)
    both = jnp.concatenate([row0, row1, jnp.zeros((14, 3 * c), F32)], 0).astype(BF16)
    return both[:, :c], both[:, c:]


def mix_kernel(parts, *refs):
    s_refs, (scale_ref, w_ref) = refs[:parts], refs[parts:parts + 2]
    o_refs, (in_ref, sum_ref, out_ref) = refs[parts + 2:-3], refs[-3:]
    mz, _, c, _ = w_ref.shape[2:]
    qx = in_ref.shape[0]
    blk, depth, width = s_refs[0].shape[1:]
    rows = 4 * mz
    a, j = pl.program_id(0), pl.program_id(1)

    @pl.when((a == 0) & (j == 0))
    def _():
        totals = []
        for s_ref in s_refs:
            total = s_ref[0].astype(F32)
            for s in range(1, s_ref.shape[0]):
                total = total + s_ref[s].astype(F32)
            totals.append(total)
        sum_ref[...] = jnp.concatenate(totals, 1).reshape(c * qx, width)
        for i in range(qx):
            in_ref[i] = sum_ref[every(i, c, qx), :].T * scale_ref[...]

    start = pl.multiple_of(a * rows, 8)
    x = in_ref[j, pl.ds(start, rows), :]
    mixed = []
    for k in range(mz):
        f2, g2 = pair_rows(x, k, c)
        wk = w_ref[0, 0, k].reshape(2 * c, c)
        fm = dot(f2, wk, ((1,), (1,)))
        gm = dot(g2, wk)
        mixed += [fm[0:1, :c] - fm[1:2, c:], fm[1:2, :c] + fm[0:1, c:], gm[0:2]]
    out_ref[j, pl.ds(start, rows), :] = jnp.concatenate(mixed, 0)

    @pl.when((a == pl.num_programs(0) - 1) & (j == pl.num_programs(1) - 1))
    def _():
        for i in range(qx):
            sum_ref[every(i, c, qx), :] = out_ref[i].T
        back = sum_ref[...].reshape(blk, parts * depth, width)
        for part, o_ref in enumerate(o_refs):
            piece = back[:, part * depth:(part + 1) * depth].astype(BF16)
            for s in range(o_ref.shape[0]):
                o_ref[s] = piece


def mix(spectra, scales, weights):
    a, b, mz, _, c, _ = weights.shape
    sent = spectra[0].shape
    width = sent[-1]
    whole = pl.BlockSpec(sent, lambda i, j: (0, 0, 0, 0))
    return pl.pallas_call(
        functools.partial(mix_kernel, len(spectra)),
        grid=(a, b),
        in_specs=[whole] * len(spectra) + [
            pl.BlockSpec(scales.shape, lambda i, j: (0, 0)),
            pl.BlockSpec((1, 1, mz, 2, c, c), lambda i, j: (i, j, 0, 0, 0, 0)),
        ],
        out_specs=[whole] * len(spectra) + [pl.BlockSpec((b, width, c), lambda i, j: (0, 0, 0))],
        out_shape=[jax.ShapeDtypeStruct(sent, BF16)] * len(spectra)
        + [jax.ShapeDtypeStruct((b, width, c), F32)],
        scratch_shapes=[
            pltpu.VMEM((c * b, width), F32),
            pltpu.VMEM((b, width, c), F32),
        ],
        compiler_params=pltpu.CompilerParams(vmem_limit_bytes=48 * 2**20),
        cost_estimate=estimate(a * b * mz * c * c * 128, 2 * weights.size),
        name="mixing",
    )(*spectra, scales, weights)


def outer_kernel(in_ref, wg_ref):
    mz, _, c, _ = wg_ref.shape[2:]
    rows = 4 * mz
    start = pl.multiple_of(pl.program_id(0) * rows, 8)
    x = in_ref[pl.program_id(1), pl.ds(start, rows), :]
    for k in range(mz):
        f2, g2 = pair_rows(x, k, c)
        wg_ref[0, 0, k] = dot(g2, f2, ((0,), (0,))).reshape(2, c, c)


def outer(spectra, shape):
    a, b, mz, _, c, _ = shape
    return pl.pallas_call(
        outer_kernel,
        grid=(a, b),
        in_specs=[pl.BlockSpec(spectra.shape, lambda i, j: (0, 0, 0))],
        out_specs=pl.BlockSpec((1, 1, mz, 2, c, c), lambda i, j: (i, j, 0, 0, 0, 0)),
        out_shape=jax.ShapeDtypeStruct(shape, F32),
        compiler_params=pltpu.CompilerParams(vmem_limit_bytes=48 * 2**20),
        cost_estimate=estimate(a * b * mz * c * c * 64, 8 * a * b * mz * c * c),
        name="weight_grad",
    )(spectra)


def synthesis_kernel(scales, m_ref, za_ref, zu_ref, tx_ref, ty_ref, *refs):
    y_ref, u_ref, t_ref, zs_ref = refs[-4:]
    groups, lanes, ny = ty_ref.shape
    half = lanes // 2
    space, blk, _, qx, width = m_ref.shape
    my = blk * qx
    per_group, mz = za_ref.shape[0], za_ref.shape[1]
    nx, mx = tx_ref.shape[0], tx_ref.shape[1] // 2
    columns = []
    for s in range(space):
        columns.append(jnp.concatenate([m_ref[s, b, 0] for b in range(blk)], 0))
    spectrum = jnp.concatenate(columns, 1)
    zs_ref[...] = jnp.concatenate([spectrum] * (half // my), 0).T
    for h, (zc_ref, o_ref) in enumerate(((za_ref, y_ref), (zu_ref, u_ref))):
        real = [zs_ref[every(4 * k + 2 * h, mx, 4 * mz), :] for k in range(mz)]
        imag = [zs_ref[every(4 * k + 2 * h + 1, mx, 4 * mz), :] for k in range(mz)]
        for j in range(per_group):
            re = im = None
            for k in range(mz):
                c = zc_ref[j, k, 0:1, :]
                s = zc_ref[j, k, 1:2, :]
                zr = real[k] * c - imag[k] * s
                zi = imag[k] * c + real[k] * s
                re = zr if k == 0 else re + zr
                im = zi if k == 0 else im + zi
            re = re * scales[h]
            im = im * scales[h]
            upper = jnp.concatenate([re, im], 1)
            lower = jnp.concatenate([-im, re], 1)
            block = jnp.concatenate([upper, lower], 0).astype(BF16)
            t_ref[h, j * nx:(j + 1) * nx, :] = dot(tx_ref[...], block).astype(BF16)
        for i in range(groups):
            out = dot(t_ref[h], ty_ref[i]).astype(BF16)
            o_ref[0, i * per_group:(i + 1) * per_group] = out.reshape(per_group, nx, ny)


def synthesize(spectra, za, zu, tx, ty, scales, channels, offset, earlier):
    space, blk, c, qx, width = spectra.shape
    per_group, mz, half = za.shape[0], za.shape[1], za.shape[-1]
    groups, _, ny = ty.shape
    nx, mx = tx.shape[0], tx.shape[1] // 2
    nz = per_group * groups
    field = pl.BlockSpec((1, nz, nx, ny), lambda i: (i + offset, 0, 0, 0))
    return pl.pallas_call(
        functools.partial(synthesis_kernel, scales),
        grid=(c,),
        in_specs=[
            pl.BlockSpec((space, blk, 1, qx, width), lambda i: (0, 0, i, 0, 0)),
            pl.BlockSpec(za.shape, lambda i: (0, 0, 0, 0)),
            pl.BlockSpec(zu.shape, lambda i: (0, 0, 0, 0)),
            pl.BlockSpec(tx.shape, lambda i: (0, 0)),
            pl.BlockSpec(ty.shape, lambda i: (0, 0, 0)),
        ] + [pl.BlockSpec(memory_space=pl.ANY)] * len(earlier),
        out_specs=[field, field],
        out_shape=[jax.ShapeDtypeStruct((channels, nz, nx, ny), BF16)] * 2,
        input_output_aliases={5 + i: i for i in range(len(earlier))},
        scratch_shapes=[
            pltpu.VMEM((2, per_group * nx, 2 * half), BF16),
            pltpu.VMEM((mx * mz * 4, half), F32),
        ],
        compiler_params=pltpu.CompilerParams(vmem_limit_bytes=48 * 2**20),
        cost_estimate=estimate(2 * c * nz * nx * ny * 2 * 256, 4 * c * nz * nx * ny),
        name="synthesis",
    )(spectra, za, zu, tx, ty, *earlier)


def shards(input_field, cotangent, weights):
    blk_count = lax.axis_size("blk")
    space_count = lax.axis_size("space")
    space_index = lax.axis_index("space")
    c_local, nz_local, nx, ny = input_field.shape
    px, qx, mz = weights.shape[:3]
    mx, my = px * space_count, qx * blk_count
    channels = c_local * blk_count
    nz = nz_local * space_count
    groups = lane_groups(my, nz_local)
    devices = space_count * blk_count
    forward_scale = 1.0 / math.sqrt(nx * ny * nz)
    synth_scale = 1.0 / math.sqrt(mx * my * mz)
    amplitude = np.where(np.arange(mz) == 0, 1.0, 2.0).astype(np.float32)
    ty_in, ty_out = y_tables(ny, my, groups)
    tx_in, tx_out = x_tables(nx, mx)
    zc_unit, zc_amp = z_tables(nz, mz, my, space_count, groups)
    zc_unit = lax.dynamic_index_in_dim(jnp.asarray(zc_unit), space_index, 0, keepdims=False)
    zc_amp = lax.dynamic_index_in_dim(jnp.asarray(zc_amp), space_index, 0, keepdims=False)
    width = px * mz * 4
    pieces = 1
    c_part = c_local // pieces
    sent = (space_count, blk_count, c_part, qx, width)
    scales = np.empty((px, mz, 2, 2, channels), np.float32)
    scales[:, :, 0] = np.float32(forward_scale)
    scales[:, :, 1] = (amplitude * np.float32(synth_scale))[None, :, None, None]
    scales = scales.reshape(width, channels)

    def exchange(send):
        return lax.all_to_all(send, ("space", "blk"), split_axis=0, concat_axis=0, tiled=True)

    got = []
    for part in range(pieces):
        own = analyse(input_field, cotangent, ty_in, tx_in, zc_unit, sent, part * c_part)
        moved = exchange(own.reshape(devices, c_part * qx, width).astype(BF16))
        got.append(moved.reshape(space_count, blk_count, c_part * qx, width))
    *back, spectra = mix(got, scales, weights)
    weight_grad = outer(spectra, weights.shape)

    outs = ()
    for part in range(pieces):
        home = exchange(back[part].reshape(devices, c_part * qx, width))
        home = home.astype(F32).reshape(sent)
        outs = synthesize(
            home, zc_amp, zc_unit, tx_out, ty_out, (synth_scale, forward_scale),
            c_local, part * c_part, outs,
        )
    return (outs[0], outs[1], weight_grad)


def solution(mesh):
    placed = (
        P("blk", "space", None, None),
        P("blk", "space", None, None),
        P("space", "blk", None, None, None, None),
    )
    return jax.shard_map(
        shards,
        mesh=mesh,
        in_specs=placed,
        out_specs=placed,
        check_vma=False,
    )
```
